128 devices in a mesh: ax: 8 (over z, core), circ: 16 (over y, x).
Axes of the slice: x: 4, y: 4, z: 4, core: 2. Of those that a mesh axis runs over, the one named last changes fastest.
Arguments:
- blocks_a: bfloat16 [64, 128, 5, 128, 128], P('ax', 'circ'), may hold values from -0.5 to 0.5
- blocks_p: bfloat16 [64, 128, 3, 128, 128], P('ax', 'circ'), may hold values from -0.5 to 0.5
- send_slot: int32 [64, 128, 3, 5, 3], P('ax', 'circ'), may hold values from 0 to 255, as said below
- recv_entry: int32 [128, 256], P(('ax', 'circ')), may hold values from 0 to 63, as said below
Outputs:
- coarse: bfloat16 [8192, 128, 128], P(('ax', 'circ'))
The draws below stay inside these ranges and needn't reach their ends.
Inputs may be any that keep to these rules, and one draw needn't show every extreme that they name: `send_slot`: all terms of one block row and one k name the same owner; a few owners are named by far more terms than the rest. `recv_entry`: each row names every value exactly 4 times.
All inputs are finite; a program needn't handle non-finite values.
Results may differ from the reference program's by a relative error of at most 0.0064.
Values may be sent and summed in bfloat16 or wider, within the bound.
A program may use at most 192 MiB of HBM per device.

```python
import jax
import jax.numpy as jnp
from jax import lax

BLOCK = 128
STENCIL = 5
KP = 3
SLOT = 2
RA = 8
RC = 8
OWNERS = 128
NRA = 64
NRC = 128
CE = 64
N_AX = 8
N_CIRC = 16


def draw_send_slot(key, part):
    key_hot = jax.random.fold_in(key, 11)
    key_pick = jax.random.fold_in(key, 12)
    key_slot = jax.random.fold_in(key, 13)
    hot_owners = jax.random.permutation(key_hot, OWNERS)[:4]
    picked = jax.random.randint(key_pick, (NRA, NRC, KP), 0, 2 * OWNERS)
    owner = jnp.where(picked < OWNERS, picked, hot_owners[picked % 4])
    within = jax.random.randint(key_slot, (NRA, NRC, KP, STENCIL, KP), 0, SLOT)
    return (owner[:, :, :, None, None] * SLOT + within).astype(jnp.int32)


def draw_recv_entry(key, part):
    keys = jax.random.split(jax.random.fold_in(key, 21), OWNERS)
    orders = jax.vmap(lambda single: jax.random.permutation(single, OWNERS * SLOT))(keys)
    return (orders % CE).astype(jnp.int32)


def levels(key, shape, cuts, smallest, top_value):
    def one(position, blocks):
        heights = jax.random.uniform(jax.random.fold_in(jax.random.fold_in(key, 6), position), (blocks,), jnp.float32, smallest / len(cuts), top_value / len(cuts))
        return jnp.repeat(jnp.exp(heights), shape[position] // blocks).reshape((-1,) + (1,) * (len(shape) - position - 1))

    loudness = one(*cuts[0])
    for cut in cuts[1:]:
        loudness = loudness * one(*cut)
    return loudness


def scatter_about(key, shape, spread, bound, shards=(), kind=jnp.bfloat16):
    loudness = levels(key, shape, shards, -0.22, 0.18) if shards else 1.0
    drawn = jax.random.normal(key, shape, jnp.float32) * spread * loudness
    return jnp.minimum(jnp.maximum(drawn, -bound), bound).astype(kind)


def setup_inputs(seed: int = 0) -> dict:
    key_of = jax.random.split(jax.random.key(seed), 5)
    blocks_a = scatter_about(key_of[0], (NRA, NRC, STENCIL, BLOCK, BLOCK), BLOCK ** -0.5, 0.5, ((0, 8), (1, 16)))
    blocks_p = scatter_about(key_of[1], (NRA, NRC, KP, BLOCK, BLOCK), BLOCK ** -0.5, 0.5, ((0, 8), (1, 16)))
    send_slot = draw_send_slot(jax.random.fold_in(key_of[4], 71), 0)
    recv_entry = draw_recv_entry(jax.random.fold_in(key_of[4], 71), 0)
    return dict(blocks_a=blocks_a, blocks_p=blocks_p, send_slot=send_slot, recv_entry=recv_entry)


def window(array_in, row_start, col_start):
    sizes = (RA, RC) + tuple(array_in.shape[2:])
    starts = (row_start, col_start) + tuple(jnp.int32(0) for _ in array_in.shape[2:])
    return lax.dynamic_slice(array_in, starts, sizes)


def source_terms(coupling, owned, nearby, slots, total_slots):
    block_width = owned.shape[-1]
    product = jnp.einsum("xyjab,xyjlbc->xyjlac", coupling.astype(jnp.float32), nearby.astype(jnp.float32)).astype(jnp.bfloat16)
    within = slots % SLOT
    picks = (within[:, :, :, None, :, :] == jnp.arange(SLOT, dtype=jnp.int32)[None, None, None, :, None, None]).astype(jnp.float32)
    gathered = jnp.einsum("xykwjl,xyjlac->xykwac", picks, product.astype(jnp.float32)).astype(jnp.bfloat16)
    terms = jnp.einsum("xykba,xykwbc->xykwac", owned.astype(jnp.float32), gathered.astype(jnp.float32))
    owner_slot = (slots[:, :, :, 0, 0] // SLOT) * SLOT
    targets = owner_slot[:, :, :, None] + jnp.arange(SLOT, dtype=jnp.int32)[None, None, None, :]
    summed = jnp.zeros((total_slots, block_width, block_width), jnp.float32)
    summed = summed.at[targets.reshape(-1)].add(terms.reshape(-1, block_width, block_width))
    return summed.astype(jnp.bfloat16)


def reference(blocks_a, blocks_p, send_slot, recv_entry):
    owners = N_AX * N_CIRC
    total_slots = owners * SLOT
    block_width = blocks_p.shape[-1]
    padded = jnp.pad(blocks_p, ((1, 1), (0, 0), (0, 0), (0, 0), (0, 0)))
    wrapped = jnp.concatenate([blocks_p[:, -1:], blocks_p, blocks_p[:, :1]], axis=1)
    slot_ids = jnp.arange(total_slots, dtype=jnp.int32)
    dest = slot_ids // SLOT
    within = slot_ids % SLOT

    def one_source(summed_coarse, source):
        row0 = ((source // N_CIRC) * RA).astype(jnp.int32)
        col0 = ((source % N_CIRC) * RC).astype(jnp.int32)
        owned = window(blocks_p, row0, col0)
        nearby = jnp.stack([owned, window(padded, row0, col0), window(padded, row0 + 2, col0),
                            window(wrapped, row0, col0), window(wrapped, row0, col0 + 2)], axis=2)
        coupling = window(blocks_a, row0, col0)
        slots = window(send_slot, row0, col0)
        partial_sum = source_terms(coupling, owned, nearby, slots, total_slots)
        target = dest * CE + recv_entry[dest, source * SLOT + within]
        summed_coarse = summed_coarse.at[target].add(partial_sum.astype(jnp.float32))
        return summed_coarse, None

    start = jnp.zeros((owners * CE, block_width, block_width), jnp.float32)
    summed_coarse, _ = lax.scan(one_source, start, jnp.arange(owners, dtype=jnp.int32))
    return summed_coarse.astype(jnp.bfloat16)
```

```python
import functools

import jax
import jax.numpy as jnp
from jax import lax
from jax.experimental import pallas as pl
from jax.experimental.pallas import tpu as pltpu
from jax.sharding import PartitionSpec as P

MESH = pl.DeviceIdType.MESH
B = 128
ROWS = 64
KP = 3
ST = 5
TASKS = ROWS * KP
OWNERS = 128
ENTRIES = 64
CHUNKS = ((0, 32), (32, 32), (64, 32), (96, 32))
STEP = 37
NT = (((1,), (1,)), ((), ()))
OFF_PERM = TASKS * ST
OFF_SAME = OFF_PERM + TASKS
OFF_LAST = OFF_SAME + TASKS
OFF_SOME = OFF_LAST + OWNERS
OFF_INV = OFF_SOME + OWNERS


def transpose_kernel(x_ref, o_ref):
    for i in range(x_ref.shape[0]):
        o_ref[i] = x_ref[i].T


def transposed(blocks, step):
    count = blocks.shape[0]
    spec = pl.BlockSpec((step, B, B), lambda i: (i, 0, 0))
    return pl.pallas_call(
        transpose_kernel,
        grid=(count // step,),
        out_shape=jax.ShapeDtypeStruct((count, B, B), jnp.bfloat16),
        in_specs=[spec],
        out_specs=spec,
        cost_estimate=pl.CostEstimate(flops=0, bytes_accessed=count * B * B * 4, transcendentals=0),
        compiler_params=pltpu.CompilerParams(vmem_limit_bytes=32 * 2**20),
    )(blocks)


def offset_device(step):
    ax, ci = lax.axis_index("ax"), lax.axis_index("circ")
    off = lax.rem(step * STEP, 128)
    core = lax.rem(ax + off, 2)
    x = lax.rem(lax.rem(ci, 4) + off // 2, 4)
    y = lax.rem(ci // 4 + off // 8, 4)
    z = lax.rem(ax // 2 + off // 32, 4)
    return z * 2 + core, y * 4 + x


def galerkin_kernel(tab, a_hbm, pt_hbm, out_ref, a_buf, px, s_buf, term, run, *rest):
    n_chunks = len(CHUNKS)
    sends, recvs = rest[:n_chunks], rest[n_chunks : 2 * n_chunks]
    a_sem, p_sem, hs_sem, hr_sem, s_sem, r_sem = rest[2 * n_chunks :]
    ax, ci = lax.axis_index("ax"), lax.axis_index("circ")
    me = ax * 16 + ci
    n_ax, n_ci = 8, 16

    a_copy = pltpu.make_async_copy(a_hbm, a_buf, a_sem)
    a_copy.start()
    p_copy = pltpu.make_async_copy(pt_hbm, px.at[pl.ds(1, 8), pl.ds(1, 8)], p_sem)
    p_copy.start()

    barrier = pltpu.get_barrier_semaphore()

    def greet(i, carry):
        pl.semaphore_signal(barrier, inc=1, device_id=offset_device(i), device_id_type=MESH)
        return carry

    lax.fori_loop(1, OWNERS, greet, 0)
    pl.semaphore_wait(barrier, OWNERS - 1)

    up, down = (lax.rem(ax + n_ax - 1, n_ax), ci), (lax.rem(ax + 1, n_ax), ci)
    left, right = (ax, lax.rem(ci + n_ci - 1, n_ci)), (ax, lax.rem(ci + 1, n_ci))
    halos = []
    for h, (c0, cw) in enumerate(CHUNKS):
        cols = pl.ds(c0, cw)
        eight = pl.ds(1, 8)
        four = (
            (pt_hbm.at[:, 0, :, cols], px.at[eight, 9, :, cols], left),
            (pt_hbm.at[:, 7, :, cols], px.at[eight, 0, :, cols], right),
            (pt_hbm.at[0, :, :, cols], px.at[9, eight, :, cols], up),
            (pt_hbm.at[7, :, :, cols], px.at[0, eight, :, cols], down),
        )
        copies = []
        for d, (src, dst, device) in enumerate(four):
            copy = pltpu.make_async_remote_copy(
                src_ref=src,
                dst_ref=dst,
                send_sem=hs_sem.at[h * 4 + d],
                recv_sem=hr_sem.at[h * 4 + d],
                device_id=device,
                device_id_type=MESH,
            )
            copy.start()
            copies.append(copy)
        halos.append(copies)

    p_copy.wait()
    a_copy.wait()

    for h, (c0, cw) in enumerate(CHUNKS):
        send, recv = sends[h], recvs[h]
        cols = pl.ds(c0, cw)
        two = 2 * cw
        for copy in halos[h]:
            copy.wait()

        @pl.when(ax == 0)
        def _():
            px[0, pl.ds(1, 8), :, cols] = jnp.zeros((8, KP, cw, B), jnp.bfloat16)

        @pl.when(ax == n_ax - 1)
        def _():
            px[9, pl.ds(1, 8), :, cols] = jnp.zeros((8, KP, cw, B), jnp.bfloat16)

        def subsets(n, carry):
            i, j = n // 10, lax.rem(n, 10)
            p0, p1, p2 = (px[i, j, l, cols] for l in range(KP))
            f0, f1, f2 = (p.astype(jnp.float32) for p in (p0, p1, p2))
            f01 = f0 + f1
            zero = jnp.zeros_like(p0)
            entries = (zero, p0, p1, f01, p2, f0 + f2, f1 + f2, f01 + f2)
            for s, value in enumerate(entries):
                s_buf[n * 8 + s, pl.ds(0, cw)] = value.astype(jnp.bfloat16)
            return carry

        lax.fori_loop(1, 99, subsets, 0)

        def row(r, carry):
            i, j = r // 8 + 1, lax.rem(r, 8) + 1
            base = i * 10 + j
            lhs = []
            for nb, d in enumerate((0, -10, 10, -1, 1)):
                at = (base + d) * 8
                parts = []
                for k in range(KP):
                    mask = tab[(r * KP + k) * ST + nb]
                    parts += [s_buf[at + mask, pl.ds(0, cw)], s_buf[at + 7 - mask, pl.ds(0, cw)]]
                lhs.append(jnp.concatenate(parts, axis=0))
            lhs = jnp.concatenate(lhs, axis=1)
            rhs = jnp.concatenate([a_buf[r * ST + nb] for nb in range(ST)], axis=1)
            gathered = lax.dot_general(lhs, rhs, NT, preferred_element_type=jnp.float32).astype(jnp.bfloat16)
            for k in range(KP):
                term[r * KP + k, pl.ds(0, two)] = lax.dot_general(
                    gathered[k * two : (k + 1) * two], px[i, j, k], NT, preferred_element_type=jnp.float32
                )
            return carry

        lax.fori_loop(0, ROWS, row, 0)

        def accumulate(i, total):
            same = tab[OFF_SAME + i].astype(jnp.float32)
            total = total * same + term[tab[OFF_PERM + i], pl.ds(0, two)]
            run[i, pl.ds(0, two)] = total.astype(jnp.bfloat16)
            return total

        lax.fori_loop(0, TASKS, accumulate, jnp.zeros((two, B), jnp.float32))

        def partial(owner):
            some = tab[OFF_SOME + owner].astype(jnp.float32)
            value = run[tab[OFF_LAST + owner], pl.ds(0, two)]
            return (value.astype(jnp.float32) * some).astype(jnp.bfloat16)

        def send_one(i, carry):
            device = offset_device(i)
            send[i] = partial(device[0] * 16 + device[1])
            pltpu.make_async_remote_copy(
                src_ref=send.at[i],
                dst_ref=recv.at[me],
                send_sem=s_sem.at[h],
                recv_sem=r_sem.at[h],
                device_id=device,
                device_id_type=MESH,
            ).start()
            return carry

        lax.fori_loop(1, OWNERS, send_one, 0)
        recv[me] = partial(me)

    for h, (c0, cw) in enumerate(CHUNKS):
        send, recv = sends[h], recvs[h]
        others = pl.ds(0, OWNERS - 1)
        pltpu.make_async_copy(recv.at[others], recv.at[others], r_sem.at[h]).wait()

        def entry(e, carry):
            total = jnp.zeros((cw, B), jnp.float32)
            for q in range(4):
                slot = tab[OFF_INV + e * 4 + q]
                total = total + recv[slot // 2, pl.ds(lax.rem(slot, 2) * cw, cw)].astype(jnp.float32)
            out_ref[e, pl.ds(c0, cw)] = total.astype(jnp.bfloat16)
            return carry

        lax.fori_loop(0, ENTRIES, entry, 0)

    for h in range(n_chunks):
        others = pl.ds(0, OWNERS - 1)
        pltpu.make_async_copy(sends[h].at[others], sends[h].at[others], s_sem.at[h]).wait()


def tables(send_slot, recv_entry):
    slots = send_slot.reshape(TASKS, ST, KP)
    weights = (1 << jnp.arange(KP, dtype=jnp.int32))[None, None, :]
    masks = jnp.sum((1 - slots % 2) * weights, axis=2).reshape(-1)
    owner = slots[:, 0, 0] // 2
    ids = jnp.arange(TASKS, dtype=jnp.int32)
    before = (owner[None, :] < owner[:, None]) | ((owner[None, :] == owner[:, None]) & (ids[None, :] < ids[:, None]))
    rank = jnp.sum(before.astype(jnp.int32), axis=1)
    place = (rank[None, :] == ids[:, None]).astype(jnp.int32)
    perm = jnp.sum(place * ids[None, :], axis=1)
    sorted_owner = jnp.sum(place * owner[None, :], axis=1)
    same = jnp.concatenate([jnp.zeros((1,), jnp.int32), (sorted_owner[1:] == sorted_owner[:-1]).astype(jnp.int32)])
    names = jnp.arange(OWNERS, dtype=jnp.int32)
    upto = jnp.sum((owner[None, :] <= names[:, None]).astype(jnp.int32), axis=1)
    some = jnp.max((owner[None, :] == names[:, None]).astype(jnp.int32), axis=1)
    last = jnp.maximum(upto - 1, 0)
    entries = recv_entry[0]
    at = jnp.arange(2 * OWNERS, dtype=jnp.int32)
    earlier = jnp.sum(((entries[None, :] == entries[:, None]) & (at[None, :] < at[:, None])).astype(jnp.int32), axis=1)
    position = entries * 4 + earlier
    inverse = jnp.sum((position[None, :] == at[:, None]).astype(jnp.int32) * at[None, :], axis=1)
    return jnp.concatenate([masks, perm, same, last, some, inverse])


def body(blocks_a, blocks_p, send_slot, recv_entry):
    tab = tables(send_slot, recv_entry)
    flipped = transposed(blocks_p.reshape(TASKS, B, B), 24).reshape(8, 8, KP, B, B)
    widest = max(cw for _, cw in CHUNKS)
    n_chunks = len(CHUNKS)
    bf16 = jnp.bfloat16
    out = pl.pallas_call(
        galerkin_kernel,
        out_shape=jax.ShapeDtypeStruct((ENTRIES, B, B), bf16),
        in_specs=[
            pl.BlockSpec(memory_space=pltpu.SMEM),
            pl.BlockSpec(memory_space=pl.ANY),
            pl.BlockSpec(memory_space=pl.ANY),
        ],
        out_specs=pl.BlockSpec(memory_space=pltpu.VMEM),
        scratch_shapes=[
            pltpu.VMEM((ROWS * ST, B, B), bf16),
            pltpu.VMEM((10, 10, KP, B, B), bf16),
            pltpu.VMEM((800, widest, B), bf16),
            pltpu.VMEM((TASKS, 2 * widest, B), jnp.float32),
            pltpu.VMEM((TASKS, 2 * widest, B), bf16),
        ]
        + [pltpu.VMEM((OWNERS, 2 * cw, B), bf16) for _, cw in CHUNKS] * 2
        + [
            pltpu.SemaphoreType.DMA,
            pltpu.SemaphoreType.DMA,
            pltpu.SemaphoreType.DMA((4 * n_chunks,)),
            pltpu.SemaphoreType.DMA((4 * n_chunks,)),
            pltpu.SemaphoreType.DMA((n_chunks,)),
            pltpu.SemaphoreType.DMA((n_chunks,)),
        ],
        cost_estimate=pl.CostEstimate(flops=16_000_000_000, bytes_accessed=30_000_000, transcendentals=0),
        compiler_params=pltpu.CompilerParams(
            collective_id=0, has_side_effects=True, vmem_limit_bytes=60 * 2**20
        ),
    )(tab, blocks_a.reshape(ROWS * ST, B, B), flipped)
    return transposed(out, 16)


def solution(mesh):
    in_specs = (
        P("ax", "circ", None, None, None),
        P("ax", "circ", None, None, None),
        P("ax", "circ", None, None, None),
        P(("ax", "circ"), None),
    )
    out_specs = P(("ax", "circ"), None, None)
    return jax.shard_map(body, mesh=mesh, in_specs=in_specs, out_specs=out_specs, check_vma=False)
```

```python
import functools

import jax
import jax.numpy as jnp
from jax import lax
from jax.experimental import pallas as pl
from jax.experimental.pallas import tpu as pltpu
from jax.sharding import PartitionSpec as P

MESH = pl.DeviceIdType.MESH
B = 128
ROWS = 64
KP = 3
ST = 5
TASKS = ROWS * KP
OWNERS = 128
ENTRIES = 64
CHUNKS = ((0, 32), (32, 32), (64, 32), (96, 32))
STEP = 37
OFF_PERM = TASKS * ST
OFF_SAME = OFF_PERM + TASKS
OFF_LAST = OFF_SAME + TASKS
OFF_SOME = OFF_LAST + OWNERS
OFF_SRC = OFF_SOME + OWNERS
OFF_WITHIN = OFF_SRC + 2 * OWNERS
BATCH_TASKS = 32
FLIPS = 20


def transpose_kernel(x_ref, o_ref):
    for i in range(x_ref.shape[0]):
        o_ref[i] = x_ref[i].T


def transposed(blocks, step):
    count = blocks.shape[0]
    spec = pl.BlockSpec((step, B, B), lambda i: (i, 0, 0))
    return pl.pallas_call(
        transpose_kernel,
        grid=(count // step,),
        out_shape=jax.ShapeDtypeStruct((count, B, B), jnp.bfloat16),
        in_specs=[spec],
        out_specs=spec,
        cost_estimate=pl.CostEstimate(flops=0, bytes_accessed=count * B * B * 4, transcendentals=0),
        compiler_params=pltpu.CompilerParams(vmem_limit_bytes=62 * 2**20),
    )(blocks)


def offset_device(step):
    ax, ci = lax.axis_index("ax"), lax.axis_index("circ")
    off = lax.rem(step * STEP, 128)
    core = lax.rem(ax + off, 2)
    x = lax.rem(ci + lax.div(off, 2), 4)
    y = lax.rem(lax.div(ci, 4) + lax.div(off, 8), 4)
    z = lax.rem(lax.div(ax, 2) + lax.div(off, 32), 4)
    return z * 2 + core, y * 4 + x


def inner(t):
    return lax.div(t, 6) + 1, lax.rem(t, 6) + 1


def ends(t):
    return 7 * lax.div(t, 8), lax.rem(t, 8)


def sides(t):
    return lax.div(t, 2) + 1, 7 * lax.rem(t, 2)


def galerkin_kernel(tab, a_hbm, p_hbm, out_hbm, out_ref, a_buf, p_buf, px, s_buf, g_buf, run, *rest):
    n_chunks = len(CHUNKS)
    sends, recvs = rest[:n_chunks], rest[n_chunks : 2 * n_chunks]
    a_sem, p_sem, o_sem, hs_sem, hr_sem, s_sem, r_sem = rest[2 * n_chunks :]
    ax, ci = lax.axis_index("ax"), lax.axis_index("circ")
    me = ax * 16 + ci
    n_ax, n_ci = 8, 16

    p_copy = pltpu.make_async_copy(p_hbm, p_buf, p_sem)
    p_copy.start()
    a_copy = pltpu.make_async_copy(a_hbm, a_buf, a_sem)
    a_copy.start()

    barrier = pltpu.get_barrier_semaphore()

    rings = [lax.rem(ax + d, n_ax) for d in range(n_ax)]
    for d in range(1, n_ax):
        pl.semaphore_signal(barrier, inc=1, device_id=(rings[d], ci), device_id_type=MESH)

    def greet(d, carry):
        other = lax.rem(ci + d, n_ci)
        for ring in rings:
            pl.semaphore_signal(barrier, inc=1, device_id=(ring, other), device_id_type=MESH)
        return carry

    lax.fori_loop(1, n_ci, greet, 0)

    p_copy.wait()

    def flip_p(place, count, size):
        def step(n, carry):
            places = [place(n * size + q) for q in range(size)]
            flipped = [p_buf[(i * 8 + j) * KP + k].T for i, j in places for k in range(KP)]
            for q, (i, j) in enumerate(places):
                for k in range(KP):
                    px[i + 1, j + 1, k] = flipped[q * KP + k]
            return carry

        lax.fori_loop(0, count // size, step, 0)

    flip_p(ends, 16, 4)
    flip_p(sides, 12, 4)

    pl.semaphore_wait(barrier, OWNERS - 1)

    up, down = (lax.rem(ax + n_ax - 1, n_ax), ci), (lax.rem(ax + 1, n_ax), ci)
    left, right = (ax, lax.rem(ci + n_ci - 1, n_ci)), (ax, lax.rem(ci + 1, n_ci))
    halos = []
    for h, (c0, cw) in enumerate(CHUNKS):
        cols = pl.ds(c0, cw)
        eight = pl.ds(1, 8)
        four = (
            (px.at[eight, 1, :, cols], px.at[eight, 9, :, cols], left),
            (px.at[eight, 8, :, cols], px.at[eight, 0, :, cols], right),
            (px.at[1, eight, :, cols], px.at[9, eight, :, cols], up),
            (px.at[8, eight, :, cols], px.at[0, eight, :, cols], down),
        )
        copies = []
        for d, (src, dst, device) in enumerate(four):
            copy = pltpu.make_async_remote_copy(
                src_ref=src,
                dst_ref=dst,
                send_sem=hs_sem.at[h * 4 + d],
                recv_sem=hr_sem.at[h * 4 + d],
                device_id=device,
                device_id_type=MESH,
            )
            copy.start()
            copies.append(copy)
        halos.append(copies)

    flip_p(inner, 36, 4)

    a_copy.wait()

    def flip_a(n, carry):
        flipped = [a_buf[n * FLIPS + q].T for q in range(FLIPS)]
        for q in range(FLIPS):
            a_buf[n * FLIPS + q] = flipped[q]
        return carry

    lax.fori_loop(0, ROWS * ST // FLIPS, flip_a, 0)

    for h, (c0, cw) in enumerate(CHUNKS):
        send, recv = sends[h], recvs[h]
        cols = pl.ds(c0, cw)
        two = 2 * cw

        def subsets(i, j):
            n = i * 10 + j
            p0, p1, p2 = (px[i, j, l, cols] for l in range(KP))
            f0, f1, f2 = (p.astype(jnp.float32) for p in (p0, p1, p2))
            f01 = f0 + f1
            zero = jnp.zeros_like(p0)
            entries = (zero, p0, p1, f01, p2, f0 + f2, f1 + f2, f01 + f2)
            for s, value in enumerate(entries):
                s_buf[n * 8 + s, pl.ds(0, cw)] = value.astype(jnp.bfloat16)

        def subsets_own(r, carry):
            subsets(lax.div(r, 8) + 1, lax.rem(r, 8) + 1)
            return carry

        lax.fori_loop(0, ROWS, subsets_own, 0, unroll=2)
        def gather(places):
            sums = []
            for i, j in places:
                r = i * 8 + j
                base = (i + 1) * 10 + j + 1
                lhs = []
                for nb, d in enumerate((0, -10, 10, -1, 1)):
                    at = (base + d) * 8
                    parts = []
                    for k in range(KP):
                        mask = tab[(r * KP + k) * ST + nb]
                        parts += [s_buf[at + mask, pl.ds(0, cw)], s_buf[at + 7 - mask, pl.ds(0, cw)]]
                    lhs.append(jnp.concatenate(parts, axis=0))
                lhs = jnp.concatenate(lhs, axis=1)
                rhs = jnp.concatenate([a_buf[r * ST + nb] for nb in range(ST)], axis=0)
                sums.append(jnp.dot(lhs, rhs, preferred_element_type=jnp.float32).astype(jnp.bfloat16))
            for (i, j), gathered in zip(places, sums):
                for k in range(KP):
                    g_buf[(i * 8 + j) * KP + k, pl.ds(0, two)] = gathered[k * two : (k + 1) * two]

        def batch(place, count, size):
            def step(n, carry):
                gather([place(n * size + q) for q in range(size)])
                return carry

            lax.fori_loop(0, count // size, step, 0)

        batch(inner, 36, 12)

        for copy in halos[h]:
            copy.wait()

        @pl.when(ax == 0)
        def _():
            px[0, pl.ds(1, 8), :, cols] = jnp.zeros((8, KP, cw, B), jnp.bfloat16)

        @pl.when(ax == n_ax - 1)
        def _():
            px[9, pl.ds(1, 8), :, cols] = jnp.zeros((8, KP, cw, B), jnp.bfloat16)

        def subsets_halo(i, carry):
            subsets(i, 0)
            subsets(i, 9)
            subsets(0, i)
            subsets(9, i)
            return carry

        lax.fori_loop(1, 9, subsets_halo, 0)

        batch(ends, 16, 8)
        batch(sides, 12, 12)

        def tasks(step, total):
            terms = []
            blank = jnp.zeros((two, B), jnp.bfloat16)
            for q in range(0, BATCH_TASKS, 2):
                gathered, owned = [], []
                for i in (step * BATCH_TASKS + q, step * BATCH_TASKS + q + 1):
                    gathered.append(g_buf[tab[OFF_PERM + i], pl.ds(0, two)])
                    owned.append(p_buf[tab[OFF_PERM + i]])
                lhs = jnp.concatenate(
                    [
                        jnp.concatenate([gathered[0], blank], axis=1),
                        jnp.concatenate([blank, gathered[1]], axis=1),
                    ],
                    axis=0,
                )
                pair = jnp.dot(lhs, jnp.concatenate(owned, axis=0), preferred_element_type=jnp.float32)
                terms += [pair[:two], pair[two:]]
            values = []
            for q in range(BATCH_TASKS):
                total = total * tab[OFF_SAME + step * BATCH_TASKS + q].astype(jnp.float32) + terms[q]
                values.append(total.astype(jnp.bfloat16))
            for q in range(BATCH_TASKS):
                run[step * BATCH_TASKS + q, pl.ds(0, two)] = values[q]
            return total

        lax.fori_loop(0, TASKS // BATCH_TASKS, tasks, jnp.zeros((two, B), jnp.float32))

        def partial(owner):
            some = tab[OFF_SOME + owner].astype(jnp.float32)
            value = run[tab[OFF_LAST + owner], pl.ds(0, two)]
            return (value.astype(jnp.float32) * some).astype(jnp.bfloat16).reshape(2, cw, B)

        def send_one(i, carry):
            device = offset_device(i)
            send[i] = partial(device[0] * 16 + device[1])
            pltpu.make_async_remote_copy(
                src_ref=send.at[i],
                dst_ref=recv.at[me],
                send_sem=s_sem.at[h],
                recv_sem=r_sem.at[h],
                device_id=device,
                device_id_type=MESH,
            ).start()
            return carry

        lax.fori_loop(1, OWNERS, send_one, 0)
        recv[me] = partial(me)

    outs = []
    for h, (c0, cw) in enumerate(CHUNKS):
        send, recv = sends[h], recvs[h]
        others = pl.ds(0, OWNERS - 1)
        pltpu.make_async_copy(recv.at[others], recv.at[others], r_sem.at[h]).wait()

        def entry(step, carry):
            totals = []
            for q in range(4):
                e = step * 4 + q
                total = jnp.zeros((cw, B), jnp.float32)
                for piece in range(4):
                    source = tab[OFF_SRC + e * 4 + piece]
                    within = tab[OFF_WITHIN + e * 4 + piece]
                    total = total + recv[source, within].astype(jnp.float32)
                totals.append(total.astype(jnp.bfloat16))
            for q in range(4):
                out_ref[step * 4 + q, pl.ds(c0, cw)] = totals[q]
            return carry

        lax.fori_loop(0, ENTRIES // 4, entry, 0)
        done = pltpu.make_async_copy(out_ref.at[:, pl.ds(c0, cw)], out_hbm.at[:, pl.ds(c0, cw)], o_sem.at[h])
        done.start()
        outs.append(done)

    for h in range(n_chunks):
        others = pl.ds(0, OWNERS - 1)
        pltpu.make_async_copy(sends[h].at[others], sends[h].at[others], s_sem.at[h]).wait()
        outs[h].wait()


def tables(send_slot, recv_entry):
    weights = (1 << jnp.arange(KP, dtype=jnp.int32))[None, None, None, None, :]
    masks = jnp.sum((1 - send_slot % 2) * weights, axis=4).reshape(-1)
    owner = (send_slot[:, :, :, 0, 0] // 2).reshape(-1)
    ids = jnp.arange(TASKS, dtype=jnp.int32)
    before = (owner[None, :] < owner[:, None]) | ((owner[None, :] == owner[:, None]) & (ids[None, :] < ids[:, None]))
    rank = jnp.sum(before.astype(jnp.int32), axis=1)
    place = (rank[None, :] == ids[:, None]).astype(jnp.int32)
    perm = jnp.sum(place * ids[None, :], axis=1)
    sorted_owner = jnp.sum(place * owner[None, :], axis=1)
    same = jnp.concatenate([jnp.zeros((1,), jnp.int32), (sorted_owner[1:] == sorted_owner[:-1]).astype(jnp.int32)])
    names = jnp.arange(OWNERS, dtype=jnp.int32)
    upto = jnp.sum((owner[None, :] <= names[:, None]).astype(jnp.int32), axis=1)
    some = jnp.max((owner[None, :] == names[:, None]).astype(jnp.int32), axis=1)
    last = jnp.maximum(upto - 1, 0)
    entries = recv_entry[0]
    at = jnp.arange(2 * OWNERS, dtype=jnp.int32)
    earlier = jnp.sum(((entries[None, :] == entries[:, None]) & (at[None, :] < at[:, None])).astype(jnp.int32), axis=1)
    position = entries * 4 + earlier
    inverse = jnp.sum((position[None, :] == at[:, None]).astype(jnp.int32) * at[None, :], axis=1)
    return jnp.concatenate(
        [masks, perm, same, last, some, inverse // 2, inverse % 2]
    )


def body(blocks_a, blocks_p, send_slot, recv_entry):
    tab = tables(send_slot, recv_entry)
    widest = max(cw for _, cw in CHUNKS)
    n_chunks = len(CHUNKS)
    bf16 = jnp.bfloat16
    out = pl.pallas_call(
        galerkin_kernel,
        out_shape=jax.ShapeDtypeStruct((ENTRIES, B, B), bf16),
        in_specs=[
            pl.BlockSpec(memory_space=pltpu.SMEM),
            pl.BlockSpec(memory_space=pl.ANY),
            pl.BlockSpec(memory_space=pl.ANY),
        ],
        out_specs=pl.BlockSpec(memory_space=pl.ANY),
        scratch_shapes=[
            pltpu.VMEM((ENTRIES, B, B), bf16),
            pltpu.VMEM((ROWS * ST, B, B), bf16),
            pltpu.VMEM((TASKS, B, B), bf16),
            pltpu.VMEM((10, 10, KP, B, B), bf16),
            pltpu.VMEM((800, widest, B), bf16),
            pltpu.VMEM((TASKS, 2 * widest, B), bf16),
            pltpu.VMEM((TASKS, 2 * widest, B), bf16),
        ]
        + [pltpu.VMEM((OWNERS, 2, cw, B), bf16) for _, cw in CHUNKS] * 2
        + [
            pltpu.SemaphoreType.DMA,
            pltpu.SemaphoreType.DMA,
            pltpu.SemaphoreType.DMA((n_chunks,)),
            pltpu.SemaphoreType.DMA((4 * n_chunks,)),
            pltpu.SemaphoreType.DMA((4 * n_chunks,)),
            pltpu.SemaphoreType.DMA((n_chunks,)),
            pltpu.SemaphoreType.DMA((n_chunks,)),
        ],
        cost_estimate=pl.CostEstimate(flops=16_000_000_000, bytes_accessed=30_000_000, transcendentals=0),
        compiler_params=pltpu.CompilerParams(
            collective_id=0, has_side_effects=True, vmem_limit_bytes=60 * 2**20
        ),
    )(tab, blocks_a.reshape(ROWS * ST, B, B), blocks_p.reshape(TASKS, B, B))
    return transposed(out, 16)


def solution(mesh):
    in_specs = (
        P("ax", "circ", None, None, None),
        P("ax", "circ", None, None, None),
        P("ax", "circ", None, None, None),
        P(("ax", "circ"), None),
    )
    out_specs = P(("ax", "circ"), None, None)
    return jax.shard_map(body, mesh=mesh, in_specs=in_specs, out_specs=out_specs, check_vma=False)
```

```python
import functools

import jax
import jax.numpy as jnp
from jax import lax
from jax.experimental import pallas as pl
from jax.experimental.pallas import tpu as pltpu
from jax.sharding import PartitionSpec as P

MESH = pl.DeviceIdType.MESH
B = 128
ROWS = 64
KP = 3
ST = 5
TASKS = ROWS * KP
OWNERS = 128
ENTRIES = 64
CHUNKS = ((0, 32), (32, 32), (64, 32), (96, 32))
STEP = 37
OFF_PERM = TASKS * ST
OFF_SAME = OFF_PERM + TASKS
OFF_LAST = OFF_SAME + TASKS
OFF_SOME = OFF_LAST + OWNERS
OFF_SRC = OFF_SOME + OWNERS
OFF_WITHIN = OFF_SRC + 2 * OWNERS
BATCH_TASKS = 32
FLIPS = 20


def transpose_kernel(x_ref, o_ref):
    for i in range(x_ref.shape[0]):
        o_ref[i] = x_ref[i].T


def transposed(blocks, step):
    count = blocks.shape[0]
    spec = pl.BlockSpec((step, B, B), lambda i: (i, 0, 0))
    return pl.pallas_call(
        transpose_kernel,
        grid=(count // step,),
        out_shape=jax.ShapeDtypeStruct((count, B, B), jnp.bfloat16),
        in_specs=[spec],
        out_specs=spec,
        cost_estimate=pl.CostEstimate(flops=0, bytes_accessed=count * B * B * 4, transcendentals=0),
        compiler_params=pltpu.CompilerParams(vmem_limit_bytes=62 * 2**20),
    )(blocks)


def offset_device(step):
    ax, ci = lax.axis_index("ax"), lax.axis_index("circ")
    off = lax.rem(step * STEP, 128)
    core = lax.rem(ax + off, 2)
    x = lax.rem(ci + lax.div(off, 2), 4)
    y = lax.rem(lax.div(ci, 4) + lax.div(off, 8), 4)
    z = lax.rem(lax.div(ax, 2) + lax.div(off, 32), 4)
    return z * 2 + core, y * 4 + x


def inner(t):
    return lax.div(t, 6) + 1, lax.rem(t, 6) + 1


def ends(t):
    return 7 * lax.div(t, 8), lax.rem(t, 8)


def sides(t):
    return lax.div(t, 2) + 1, 7 * lax.rem(t, 2)


def galerkin_kernel(tab, a_hbm, p_hbm, out_hbm, out_ref, a_buf, p_buf, px, s_buf, g_buf, run, *rest):
    n_chunks = len(CHUNKS)
    sends, recvs = rest[:n_chunks], rest[n_chunks : 2 * n_chunks]
    a_sem, p_sem, o_sem, hs_sem, hr_sem, s_sem, r_sem = rest[2 * n_chunks :]
    ax, ci = lax.axis_index("ax"), lax.axis_index("circ")
    me = ax * 16 + ci
    n_ax, n_ci = 8, 16

    p_copies = []
    for d, (first, count) in enumerate(((0, 8), (56, 8), (8, 24), (32, 24))):
        part = pl.ds(first * KP, count * KP)
        copy = pltpu.make_async_copy(p_hbm.at[part], p_buf.at[part], p_sem.at[d])
        copy.start()
        p_copies.append(copy)
    a_copy = pltpu.make_async_copy(a_hbm, a_buf, a_sem)

    barrier = pltpu.get_barrier_semaphore()

    rings = [lax.rem(ax + d, n_ax) for d in range(n_ax)]
    for d in range(1, n_ax):
        pl.semaphore_signal(barrier, inc=1, device_id=(rings[d], ci), device_id_type=MESH)

    def greet(d, carry):
        other = lax.rem(ci + d, n_ci)
        for ring in rings:
            pl.semaphore_signal(barrier, inc=1, device_id=(ring, other), device_id_type=MESH)
        return carry

    lax.fori_loop(1, n_ci, greet, 0)

    p_copies[0].wait()
    p_copies[1].wait()
    a_copy.start()

    def flip_p(place, count, size):
        def step(n, carry):
            places = [place(n * size + q) for q in range(size)]
            flipped = [p_buf[(i * 8 + j) * KP + k].T for i, j in places for k in range(KP)]
            for q, (i, j) in enumerate(places):
                for k in range(KP):
                    px[i + 1, j + 1, k] = flipped[q * KP + k]
            return carry

        lax.fori_loop(0, count // size, step, 0)

    flip_p(ends, 16, 4)
    p_copies[2].wait()
    p_copies[3].wait()
    flip_p(sides, 12, 4)

    pl.semaphore_wait(barrier, OWNERS - 1)

    up, down = (lax.rem(ax + n_ax - 1, n_ax), ci), (lax.rem(ax + 1, n_ax), ci)
    left, right = (ax, lax.rem(ci + n_ci - 1, n_ci)), (ax, lax.rem(ci + 1, n_ci))
    halos = []
    for h, (c0, cw) in enumerate(CHUNKS):
        cols = pl.ds(c0, cw)
        eight = pl.ds(1, 8)
        four = (
            (px.at[eight, 1, :, cols], px.at[eight, 9, :, cols], left),
            (px.at[eight, 8, :, cols], px.at[eight, 0, :, cols], right),
            (px.at[1, eight, :, cols], px.at[9, eight, :, cols], up),
            (px.at[8, eight, :, cols], px.at[0, eight, :, cols], down),
        )
        copies = []
        for d, (src, dst, device) in enumerate(four):
            copy = pltpu.make_async_remote_copy(
                src_ref=src,
                dst_ref=dst,
                send_sem=hs_sem.at[h * 4 + d],
                recv_sem=hr_sem.at[h * 4 + d],
                device_id=device,
                device_id_type=MESH,
            )
            copy.start()
            copies.append(copy)
        halos.append(copies)

    flip_p(inner, 36, 4)

    a_copy.wait()

    def subsets(i, j, cols, cw):
        n = i * 10 + j
        p0, p1, p2 = (px[i, j, l, cols] for l in range(KP))
        f0, f1, f2 = (p.astype(jnp.float32) for p in (p0, p1, p2))
        f01 = f0 + f1
        zero = jnp.zeros_like(p0)
        entries = (zero, p0, p1, f01, p2, f0 + f2, f1 + f2, f01 + f2)
        for s, value in enumerate(entries):
            s_buf[n * 8 + s, pl.ds(0, cw)] = value.astype(jnp.bfloat16)

    def flip_a(n, carry):
        flipped = [a_buf[n * FLIPS + q].T for q in range(FLIPS)]
        for q in range(4):
            r = n * 4 + q
            subsets(lax.div(r, 8) + 1, lax.rem(r, 8) + 1, pl.ds(*CHUNKS[0]), CHUNKS[0][1])
        for q in range(FLIPS):
            a_buf[n * FLIPS + q] = flipped[q]
        return carry

    lax.fori_loop(0, ROWS * ST // FLIPS, flip_a, 0)

    for h, (c0, cw) in enumerate(CHUNKS):
        send, recv = sends[h], recvs[h]
        cols = pl.ds(c0, cw)
        two = 2 * cw

        def subsets_own(r, carry):
            subsets(lax.div(r, 8) + 1, lax.rem(r, 8) + 1, cols, cw)
            return carry

        if h > 0:
            lax.fori_loop(0, ROWS, subsets_own, 0, unroll=2)

        def gather(places):
            sums = []
            for i, j in places:
                r = i * 8 + j
                base = (i + 1) * 10 + j + 1
                lhs = []
                for nb, d in enumerate((0, -10, 10, -1, 1)):
                    at = (base + d) * 8
                    parts = []
                    for k in range(KP):
                        mask = tab[(r * KP + k) * ST + nb]
                        parts += [s_buf[at + mask, pl.ds(0, cw)], s_buf[at + 7 - mask, pl.ds(0, cw)]]
                    lhs.append(jnp.concatenate(parts, axis=0))
                lhs = jnp.concatenate(lhs, axis=1)
                rhs = jnp.concatenate([a_buf[r * ST + nb] for nb in range(ST)], axis=0)
                sums.append(jnp.dot(lhs, rhs, preferred_element_type=jnp.float32).astype(jnp.bfloat16))
            for (i, j), gathered in zip(places, sums):
                for k in range(KP):
                    g_buf[(i * 8 + j) * KP + k, pl.ds(0, two)] = gathered[k * two : (k + 1) * two]

        def batch(place, count, size):
            def step(n, carry):
                gather([place(n * size + q) for q in range(size)])
                return carry

            lax.fori_loop(0, count // size, step, 0)

        batch(inner, 36, 12)

        for copy in halos[h]:
            copy.wait()

        @pl.when(ax == 0)
        def _():
            px[0, pl.ds(1, 8), :, cols] = jnp.zeros((8, KP, cw, B), jnp.bfloat16)

        @pl.when(ax == n_ax - 1)
        def _():
            px[9, pl.ds(1, 8), :, cols] = jnp.zeros((8, KP, cw, B), jnp.bfloat16)

        def subsets_halo(i, carry):
            subsets(i, 0, cols, cw)
            subsets(i, 9, cols, cw)
            subsets(0, i, cols, cw)
            subsets(9, i, cols, cw)
            return carry

        lax.fori_loop(1, 9, subsets_halo, 0)

        batch(ends, 16, 8)
        batch(sides, 12, 12)

        def tasks(step, total):
            terms = []
            blank = jnp.zeros((two, B), jnp.bfloat16)
            for q in range(0, BATCH_TASKS, 2):
                gathered, owned = [], []
                for i in (step * BATCH_TASKS + q, step * BATCH_TASKS + q + 1):
                    gathered.append(g_buf[tab[OFF_PERM + i], pl.ds(0, two)])
                    owned.append(p_buf[tab[OFF_PERM + i]])
                lhs = jnp.concatenate(
                    [
                        jnp.concatenate([gathered[0], blank], axis=1),
                        jnp.concatenate([blank, gathered[1]], axis=1),
                    ],
                    axis=0,
                )
                pair = jnp.dot(lhs, jnp.concatenate(owned, axis=0), preferred_element_type=jnp.float32)
                terms += [pair[:two], pair[two:]]
            values = []
            for q in range(BATCH_TASKS):
                total = total * tab[OFF_SAME + step * BATCH_TASKS + q].astype(jnp.float32) + terms[q]
                values.append(total.astype(jnp.bfloat16))
            for q in range(BATCH_TASKS):
                run[step * BATCH_TASKS + q, pl.ds(0, two)] = values[q]
            return total

        lax.fori_loop(0, TASKS // BATCH_TASKS, tasks, jnp.zeros((two, B), jnp.float32))

        def partial(owner):
            some = tab[OFF_SOME + owner].astype(jnp.float32)
            value = run[tab[OFF_LAST + owner], pl.ds(0, two)]
            return (value.astype(jnp.float32) * some).astype(jnp.bfloat16).reshape(2, cw, B)

        def send_one(i, carry):
            device = offset_device(i)
            send[i] = partial(device[0] * 16 + device[1])
            pltpu.make_async_remote_copy(
                src_ref=send.at[i],
                dst_ref=recv.at[me],
                send_sem=s_sem.at[h],
                recv_sem=r_sem.at[h],
                device_id=device,
                device_id_type=MESH,
            ).start()
            return carry

        lax.fori_loop(1, OWNERS, send_one, 0)
        recv[me] = partial(me)

    outs = []
    for h, (c0, cw) in enumerate(CHUNKS):
        send, recv = sends[h], recvs[h]
        others = pl.ds(0, OWNERS - 1)
        pltpu.make_async_copy(recv.at[others], recv.at[others], r_sem.at[h]).wait()

        def entry(step, carry):
            totals = []
            for q in range(4):
                e = step * 4 + q
                total = jnp.zeros((cw, B), jnp.float32)
                for piece in range(4):
                    source = tab[OFF_SRC + e * 4 + piece]
                    within = tab[OFF_WITHIN + e * 4 + piece]
                    total = total + recv[source, within].astype(jnp.float32)
                totals.append(total.astype(jnp.bfloat16))
            for q in range(4):
                out_ref[step * 4 + q, pl.ds(c0, cw)] = totals[q]
            return carry

        lax.fori_loop(0, ENTRIES // 4, entry, 0)
        done = pltpu.make_async_copy(out_ref.at[:, pl.ds(c0, cw)], out_hbm.at[:, pl.ds(c0, cw)], o_sem.at[h])
        done.start()
        outs.append(done)

    for h in range(n_chunks):
        others = pl.ds(0, OWNERS - 1)
        pltpu.make_async_copy(sends[h].at[others], sends[h].at[others], s_sem.at[h]).wait()
        outs[h].wait()


def tables(send_slot, recv_entry):
    weights = (1 << jnp.arange(KP, dtype=jnp.int32))[None, None, None, None, :]
    masks = jnp.sum((1 - send_slot % 2) * weights, axis=4).reshape(-1)
    owner = (send_slot[:, :, :, 0, 0] // 2).reshape(-1)
    ids = jnp.arange(TASKS, dtype=jnp.int32)
    before = (owner[None, :] < owner[:, None]) | ((owner[None, :] == owner[:, None]) & (ids[None, :] < ids[:, None]))
    rank = jnp.sum(before.astype(jnp.int32), axis=1)
    place = (rank[None, :] == ids[:, None]).astype(jnp.int32)
    perm = jnp.sum(place * ids[None, :], axis=1)
    sorted_owner = jnp.sum(place * owner[None, :], axis=1)
    same = jnp.concatenate([jnp.zeros((1,), jnp.int32), (sorted_owner[1:] == sorted_owner[:-1]).astype(jnp.int32)])
    names = jnp.arange(OWNERS, dtype=jnp.int32)
    upto = jnp.sum((owner[None, :] <= names[:, None]).astype(jnp.int32), axis=1)
    some = jnp.max((owner[None, :] == names[:, None]).astype(jnp.int32), axis=1)
    last = jnp.maximum(upto - 1, 0)
    entries = recv_entry[0]
    at = jnp.arange(2 * OWNERS, dtype=jnp.int32)
    same_entry = (entries[None, :] == entries[:, None]) & (at[None, :] < at[:, None])
    own_entry = jnp.where(at[None, :] == at[:, None], 4 * entries[None, :], 0)
    position = jnp.sum(same_entry.astype(jnp.int32) + own_entry, axis=1)
    inverse = jnp.sum((position[None, :] == at[:, None]).astype(jnp.int32) * at[None, :], axis=1)
    return jnp.concatenate(
        [masks, perm, same, last, some, inverse // 2, inverse % 2]
    )


def body(blocks_a, blocks_p, send_slot, recv_entry):
    tab = tables(send_slot, recv_entry)
    widest = max(cw for _, cw in CHUNKS)
    n_chunks = len(CHUNKS)
    bf16 = jnp.bfloat16
    out = pl.pallas_call(
        galerkin_kernel,
        out_shape=jax.ShapeDtypeStruct((ENTRIES, B, B), bf16),
        in_specs=[
            pl.BlockSpec(memory_space=pltpu.SMEM),
            pl.BlockSpec(memory_space=pl.ANY),
            pl.BlockSpec(memory_space=pl.ANY),
        ],
        out_specs=pl.BlockSpec(memory_space=pl.ANY),
        scratch_shapes=[
            pltpu.VMEM((ENTRIES, B, B), bf16),
            pltpu.VMEM((ROWS * ST, B, B), bf16),
            pltpu.VMEM((TASKS, B, B), bf16),
            pltpu.VMEM((10, 10, KP, B, B), bf16),
            pltpu.VMEM((800, widest, B), bf16),
            pltpu.VMEM((TASKS, 2 * widest, B), bf16),
            pltpu.VMEM((TASKS, 2 * widest, B), bf16),
        ]
        + [pltpu.VMEM((OWNERS, 2, cw, B), bf16) for _, cw in CHUNKS] * 2
        + [
            pltpu.SemaphoreType.DMA,
            pltpu.SemaphoreType.DMA((4,)),
            pltpu.SemaphoreType.DMA((n_chunks,)),
            pltpu.SemaphoreType.DMA((4 * n_chunks,)),
            pltpu.SemaphoreType.DMA((4 * n_chunks,)),
            pltpu.SemaphoreType.DMA((n_chunks,)),
            pltpu.SemaphoreType.DMA((n_chunks,)),
        ],
        cost_estimate=pl.CostEstimate(flops=16_000_000_000, bytes_accessed=30_000_000, transcendentals=0),
        compiler_params=pltpu.CompilerParams(
            collective_id=0, has_side_effects=True, vmem_limit_bytes=60 * 2**20
        ),
    )(tab, blocks_a.reshape(ROWS * ST, B, B), blocks_p.reshape(TASKS, B, B))
    return transposed(out, 32)


def solution(mesh):
    in_specs = (
        P("ax", "circ", None, None, None),
        P("ax", "circ", None, None, None),
        P("ax", "circ", None, None, None),
        P(("ax", "circ"), None),
    )
    out_specs = P(("ax", "circ"), None, None)
    return jax.shard_map(body, mesh=mesh, in_specs=in_specs, out_specs=out_specs, check_vma=False)
```

```python
import functools

import jax
import jax.numpy as jnp
from jax import lax
from jax.experimental import pallas as pl
from jax.experimental.pallas import tpu as pltpu
from jax.sharding import PartitionSpec as P

MESH = pl.DeviceIdType.MESH
B = 128
ROWS = 64
KP = 3
ST = 5
TASKS = ROWS * KP
OWNERS = 128
ENTRIES = 64
CHUNKS = ((0, 32), (32, 32), (64, 32), (96, 32))
STEP = 37
OFF_PERM = 0
OFF_SAME = OFF_PERM + TASKS
OFF_LAST = OFF_SAME + TASKS
OFF_SOME = OFF_LAST + OWNERS
OFF_SRC = OFF_SOME + OWNERS
OFF_WITHIN = OFF_SRC + 2 * OWNERS
BATCH_TASKS = 32
FLIPS = 20


def transpose_kernel(x_ref, o_ref):
    for i in range(x_ref.shape[0]):
        o_ref[i] = x_ref[i].T


def transposed(blocks, step):
    count = blocks.shape[0]
    spec = pl.BlockSpec((step, B, B), lambda i: (i, 0, 0))
    return pl.pallas_call(
        transpose_kernel,
        grid=(count // step,),
        out_shape=jax.ShapeDtypeStruct((count, B, B), jnp.bfloat16),
        in_specs=[spec],
        out_specs=spec,
        cost_estimate=pl.CostEstimate(flops=0, bytes_accessed=count * B * B * 4, transcendentals=0),
        compiler_params=pltpu.CompilerParams(vmem_limit_bytes=62 * 2**20),
    )(blocks)


def offset_device(step):
    ax, ci = lax.axis_index("ax"), lax.axis_index("circ")
    off = lax.rem(step * STEP, 128)
    core = lax.rem(ax + off, 2)
    x = lax.rem(ci + lax.div(off, 2), 4)
    y = lax.rem(lax.div(ci, 4) + lax.div(off, 8), 4)
    z = lax.rem(lax.div(ax, 2) + lax.div(off, 32), 4)
    return z * 2 + core, y * 4 + x


def inner(t):
    return lax.div(t, 6) + 1, lax.rem(t, 6) + 1


def ends(t):
    return 7 * lax.div(t, 8), lax.rem(t, 8)


def sides(t):
    return lax.div(t, 2) + 1, 7 * lax.rem(t, 2)


def galerkin_kernel(picks, tab, a_hbm, p_hbm, out_hbm, out_ref, a_buf, p_buf, px, s_buf, g_buf, run, *rest):
    n_chunks = len(CHUNKS)
    sends, recvs = rest[:n_chunks], rest[n_chunks : 2 * n_chunks]
    a_sem, p_sem, o_sem, hs_sem, hr_sem, s_sem, r_sem = rest[2 * n_chunks :]
    ax, ci = lax.axis_index("ax"), lax.axis_index("circ")
    me = ax * 16 + ci
    n_ax, n_ci = 8, 16

    p_copies = []
    for d, (first, count) in enumerate(((0, 8), (56, 8), (8, 24), (32, 24))):
        part = pl.ds(first * KP, count * KP)
        copy = pltpu.make_async_copy(p_hbm.at[part], p_buf.at[part], p_sem.at[d])
        copy.start()
        p_copies.append(copy)
    a_copy = pltpu.make_async_copy(a_hbm, a_buf, a_sem)

    barrier = pltpu.get_barrier_semaphore()

    rings = [lax.rem(ax + d, n_ax) for d in range(n_ax)]
    for d in range(1, n_ax):
        pl.semaphore_signal(barrier, inc=1, device_id=(rings[d], ci), device_id_type=MESH)

    def greet(d, carry):
        other = lax.rem(ci + d, n_ci)
        for ring in rings:
            pl.semaphore_signal(barrier, inc=1, device_id=(ring, other), device_id_type=MESH)
        return carry

    lax.fori_loop(1, n_ci, greet, 0)

    p_copies[0].wait()
    p_copies[1].wait()
    a_copy.start()

    def flip_p(place, count, size):
        def step(n, carry):
            places = [place(n * size + q) for q in range(size)]
            flipped = [p_buf[(i * 8 + j) * KP + k].T for i, j in places for k in range(KP)]
            for q, (i, j) in enumerate(places):
                for k in range(KP):
                    px[i + 1, j + 1, k] = flipped[q * KP + k]
            return carry

        lax.fori_loop(0, count // size, step, 0)

    flip_p(ends, 16, 4)
    p_copies[2].wait()
    p_copies[3].wait()
    flip_p(sides, 12, 4)

    pl.semaphore_wait(barrier, OWNERS - 1)

    up, down = (lax.rem(ax + n_ax - 1, n_ax), ci), (lax.rem(ax + 1, n_ax), ci)
    left, right = (ax, lax.rem(ci + n_ci - 1, n_ci)), (ax, lax.rem(ci + 1, n_ci))
    halos = []
    for h, (c0, cw) in enumerate(CHUNKS):
        cols = pl.ds(c0, cw)
        eight = pl.ds(1, 8)
        four = (
            (px.at[eight, 1, :, cols], px.at[eight, 9, :, cols], left),
            (px.at[eight, 8, :, cols], px.at[eight, 0, :, cols], right),
            (px.at[1, eight, :, cols], px.at[9, eight, :, cols], up),
            (px.at[8, eight, :, cols], px.at[0, eight, :, cols], down),
        )
        copies = []
        for d, (src, dst, device) in enumerate(four):
            copy = pltpu.make_async_remote_copy(
                src_ref=src,
                dst_ref=dst,
                send_sem=hs_sem.at[h * 4 + d],
                recv_sem=hr_sem.at[h * 4 + d],
                device_id=device,
                device_id_type=MESH,
            )
            copy.start()
            copies.append(copy)
        halos.append(copies)

    flip_p(inner, 36, 4)

    a_copy.wait()

    def subsets(i, j, cols, cw):
        n = i * 10 + j
        p0, p1, p2 = (px[i, j, l, cols] for l in range(KP))
        f0, f1, f2 = (p.astype(jnp.float32) for p in (p0, p1, p2))
        f01 = f0 + f1
        zero = jnp.zeros_like(p0)
        entries = (zero, p0, p1, f01, p2, f0 + f2, f1 + f2, f01 + f2)
        for s, value in enumerate(entries):
            s_buf[n * 8 + s, pl.ds(0, cw)] = value.astype(jnp.bfloat16)

    def flip_a(n, carry):
        flipped = [a_buf[n * FLIPS + q].T for q in range(FLIPS)]
        for q in range(4):
            r = n * 4 + q
            subsets(lax.div(r, 8) + 1, lax.rem(r, 8) + 1, pl.ds(*CHUNKS[0]), CHUNKS[0][1])
        for q in range(FLIPS):
            a_buf[n * FLIPS + q] = flipped[q]
        return carry

    lax.fori_loop(0, ROWS * ST // FLIPS, flip_a, 0)

    for h, (c0, cw) in enumerate(CHUNKS):
        send, recv = sends[h], recvs[h]
        cols = pl.ds(c0, cw)
        two = 2 * cw

        def subsets_own(r, carry):
            subsets(lax.div(r, 8) + 1, lax.rem(r, 8) + 1, cols, cw)
            return carry

        if h > 0:
            lax.fori_loop(0, ROWS, subsets_own, 0, unroll=2)

        def gather(places):
            sums = []
            for i, j in places:
                r = i * 8 + j
                base = (i + 1) * 10 + j + 1
                lhs = []
                for nb, d in enumerate((0, -10, 10, -1, 1)):
                    at = (base + d) * 8
                    parts = []
                    for k in range(KP):
                        mask = picks[(r * KP + k) * ST + nb]
                        parts += [s_buf[at + mask, pl.ds(0, cw)], s_buf[at + 7 - mask, pl.ds(0, cw)]]
                    lhs.append(jnp.concatenate(parts, axis=0))
                lhs = jnp.concatenate(lhs, axis=1)
                rhs = jnp.concatenate([a_buf[r * ST + nb] for nb in range(ST)], axis=0)
                sums.append(jnp.dot(lhs, rhs, preferred_element_type=jnp.float32).astype(jnp.bfloat16))
            for (i, j), gathered in zip(places, sums):
                for k in range(KP):
                    g_buf[(i * 8 + j) * KP + k, pl.ds(0, two)] = gathered[k * two : (k + 1) * two]

        def batch(place, count, size):
            def step(n, carry):
                gather([place(n * size + q) for q in range(size)])
                return carry

            lax.fori_loop(0, count // size, step, 0)

        batch(inner, 36, 12)

        for copy in halos[h]:
            copy.wait()

        @pl.when(ax == 0)
        def _():
            px[0, pl.ds(1, 8), :, cols] = jnp.zeros((8, KP, cw, B), jnp.bfloat16)

        @pl.when(ax == n_ax - 1)
        def _():
            px[9, pl.ds(1, 8), :, cols] = jnp.zeros((8, KP, cw, B), jnp.bfloat16)

        def subsets_halo(i, carry):
            subsets(i, 0, cols, cw)
            subsets(i, 9, cols, cw)
            subsets(0, i, cols, cw)
            subsets(9, i, cols, cw)
            return carry

        lax.fori_loop(1, 9, subsets_halo, 0)

        batch(ends, 16, 8)
        batch(sides, 12, 12)

        def tasks(step, total):
            terms = []
            blank = jnp.zeros((two, B), jnp.bfloat16)
            for q in range(0, BATCH_TASKS, 2):
                gathered, owned = [], []
                for i in (step * BATCH_TASKS + q, step * BATCH_TASKS + q + 1):
                    gathered.append(g_buf[tab[OFF_PERM + i], pl.ds(0, two)])
                    owned.append(p_buf[tab[OFF_PERM + i]])
                lhs = jnp.concatenate(
                    [
                        jnp.concatenate([gathered[0], blank], axis=1),
                        jnp.concatenate([blank, gathered[1]], axis=1),
                    ],
                    axis=0,
                )
                pair = jnp.dot(lhs, jnp.concatenate(owned, axis=0), preferred_element_type=jnp.float32)
                terms += [pair[:two], pair[two:]]
            values = []
            for q in range(BATCH_TASKS):
                total = total * tab[OFF_SAME + step * BATCH_TASKS + q].astype(jnp.float32) + terms[q]
                values.append(total.astype(jnp.bfloat16))
            for q in range(BATCH_TASKS):
                run[step * BATCH_TASKS + q, pl.ds(0, two)] = values[q]
            return total

        lax.fori_loop(0, TASKS // BATCH_TASKS, tasks, jnp.zeros((two, B), jnp.float32))

        def partial(owner):
            some = tab[OFF_SOME + owner].astype(jnp.float32)
            value = run[tab[OFF_LAST + owner], pl.ds(0, two)]
            return (value.astype(jnp.float32) * some).astype(jnp.bfloat16).reshape(2, cw, B)

        def send_one(i, carry):
            device = offset_device(i)
            send[i] = partial(device[0] * 16 + device[1])
            pltpu.make_async_remote_copy(
                src_ref=send.at[i],
                dst_ref=recv.at[me],
                send_sem=s_sem.at[h],
                recv_sem=r_sem.at[h],
                device_id=device,
                device_id_type=MESH,
            ).start()
            return carry

        lax.fori_loop(1, OWNERS, send_one, 0)
        recv[me] = partial(me)

    outs = []
    for h, (c0, cw) in enumerate(CHUNKS):
        send, recv = sends[h], recvs[h]
        others = pl.ds(0, OWNERS - 1)
        pltpu.make_async_copy(recv.at[others], recv.at[others], r_sem.at[h]).wait()

        def entry(step, carry):
            totals = []
            for q in range(4):
                e = step * 4 + q
                total = jnp.zeros((cw, B), jnp.float32)
                for piece in range(4):
                    source = tab[OFF_SRC + e * 4 + piece]
                    within = tab[OFF_WITHIN + e * 4 + piece]
                    total = total + recv[source, within].astype(jnp.float32)
                totals.append(total.astype(jnp.bfloat16))
            for q in range(4):
                out_ref[step * 4 + q, pl.ds(c0, cw)] = totals[q]
            return carry

        lax.fori_loop(0, ENTRIES // 4, entry, 0)
        done = pltpu.make_async_copy(out_ref.at[:, pl.ds(c0, cw)], out_hbm.at[:, pl.ds(c0, cw)], o_sem.at[h])
        done.start()
        outs.append(done)

    for h in range(n_chunks):
        others = pl.ds(0, OWNERS - 1)
        pltpu.make_async_copy(sends[h].at[others], sends[h].at[others], s_sem.at[h]).wait()
        outs[h].wait()


def tables(send_slot, recv_entry):
    weights = (1 << jnp.arange(KP, dtype=jnp.int32))[None, None, None, None, :]
    masks = jnp.sum((1 - send_slot % 2) * weights, axis=4).reshape(-1)
    owner = (send_slot[:, :, :, 0, 0] // 2).reshape(-1)
    ids = jnp.arange(TASKS, dtype=jnp.int32)
    before = (owner[None, :] < owner[:, None]) | ((owner[None, :] == owner[:, None]) & (ids[None, :] < ids[:, None]))
    rank = jnp.sum(before.astype(jnp.int32), axis=1)
    place = (rank[None, :] == ids[:, None]).astype(jnp.int32)
    perm = jnp.sum(place * ids[None, :], axis=1)
    sorted_owner = jnp.sum(place * owner[None, :], axis=1)
    same = jnp.concatenate([jnp.zeros((1,), jnp.int32), (sorted_owner[1:] == sorted_owner[:-1]).astype(jnp.int32)])
    names = jnp.arange(OWNERS, dtype=jnp.int32)
    upto = jnp.sum((owner[None, :] <= names[:, None]).astype(jnp.int32), axis=1)
    some = jnp.max((owner[None, :] == names[:, None]).astype(jnp.int32), axis=1)
    last = jnp.maximum(upto - 1, 0)
    entries = recv_entry[0]
    at = jnp.arange(2 * OWNERS, dtype=jnp.int32)
    same_entry = (entries[None, :] == entries[:, None]) & (at[None, :] < at[:, None])
    own_entry = jnp.where(at[None, :] == at[:, None], 4 * entries[None, :], 0)
    position = jnp.sum(same_entry.astype(jnp.int32) + own_entry, axis=1)
    inverse = jnp.sum((position[None, :] == at[:, None]).astype(jnp.int32) * at[None, :], axis=1)
    return masks, jnp.concatenate(
        [perm, same, last, some, inverse // 2, inverse % 2]
    )


def body(blocks_a, blocks_p, send_slot, recv_entry):
    picks, tab = tables(send_slot, recv_entry)
    widest = max(cw for _, cw in CHUNKS)
    n_chunks = len(CHUNKS)
    bf16 = jnp.bfloat16
    out = pl.pallas_call(
        galerkin_kernel,
        out_shape=jax.ShapeDtypeStruct((ENTRIES, B, B), bf16),
        in_specs=[
            pl.BlockSpec(memory_space=pltpu.SMEM),
            pl.BlockSpec(memory_space=pltpu.SMEM),
            pl.BlockSpec(memory_space=pl.ANY),
            pl.BlockSpec(memory_space=pl.ANY),
        ],
        out_specs=pl.BlockSpec(memory_space=pl.ANY),
        scratch_shapes=[
            pltpu.VMEM((ENTRIES, B, B), bf16),
            pltpu.VMEM((ROWS * ST, B, B), bf16),
            pltpu.VMEM((TASKS, B, B), bf16),
            pltpu.VMEM((10, 10, KP, B, B), bf16),
            pltpu.VMEM((800, widest, B), bf16),
            pltpu.VMEM((TASKS, 2 * widest, B), bf16),
            pltpu.VMEM((TASKS, 2 * widest, B), bf16),
        ]
        + [pltpu.VMEM((OWNERS, 2, cw, B), bf16) for _, cw in CHUNKS] * 2
        + [
            pltpu.SemaphoreType.DMA,
            pltpu.SemaphoreType.DMA((4,)),
            pltpu.SemaphoreType.DMA((n_chunks,)),
            pltpu.SemaphoreType.DMA((4 * n_chunks,)),
            pltpu.SemaphoreType.DMA((4 * n_chunks,)),
            pltpu.SemaphoreType.DMA((n_chunks,)),
            pltpu.SemaphoreType.DMA((n_chunks,)),
        ],
        cost_estimate=pl.CostEstimate(flops=16_000_000_000, bytes_accessed=30_000_000, transcendentals=0),
        compiler_params=pltpu.CompilerParams(
            collective_id=0, has_side_effects=True, vmem_limit_bytes=60 * 2**20
        ),
    )(picks, tab, blocks_a.reshape(ROWS * ST, B, B), blocks_p.reshape(TASKS, B, B))
    return transposed(out, 64)


def solution(mesh):
    in_specs = (
        P("ax", "circ", None, None, None),
        P("ax", "circ", None, None, None),
        P("ax", "circ", None, None, None),
        P(("ax", "circ"), None),
    )
    out_specs = P(("ax", "circ"), None, None)
    return jax.shard_map(body, mesh=mesh, in_specs=in_specs, out_specs=out_specs, check_vma=False)
```
